32 devices in a mesh: dp: 2 (over y), place: 16 (over z, x, core).
Axes of the slice: x: 2, y: 2, z: 4, core: 2. Of those that a mesh axis runs over, the one named last changes fastest.
Arguments:
- tokens: bfloat16 [2, 16, 256, 2048], P('dp', 'place'), may hold values from -6 to 6
- hidden_grad: bfloat16 [2, 16, 256, 256], P('dp', 'place'), may hold values from -6 to 6
- routing: int32 [2, 16, 4, 64], P('dp', 'place'), may hold values from 0 to 63, each once within a row
- row_count: int32 [2, 16], replicated, may hold values from 1 to 256, as said below
- old_slots: int32 [16], replicated, may hold values from 0 to 3, as said below
- new_slots: int32 [16], replicated, may hold values from 0 to 3, as said below
- master: float32 [4, 2048, 512], P(None, ('dp', 'place')), may hold values from -0.125 to 0.125
- first_moment: float32 [4, 2048, 512], P(None, ('dp', 'place')), may hold values from -0.018 to 0.018
- second_moment: float32 [4, 2048, 512], P(None, ('dp', 'place')), may hold values from 1e-06 to 0.0001
Outputs:
- new_weights: bfloat16 [16, 2048, 512], P('place')
- new_master: float32 [4, 2048, 512], P(None, ('dp', 'place'))
- new_first: float32 [4, 2048, 512], P(None, ('dp', 'place'))
- new_second: float32 [4, 2048, 512], P(None, ('dp', 'place'))
The draws below stay inside these ranges and needn't reach their ends.
Inputs may be any that keep to these rules, and one draw needn't show every extreme that they name: `old_slots`: every expert 0 .. 3 holds at least one slot. `new_slots`: every expert 0 .. 3 holds at least one slot. The first row_count[d, p] of a device's 256 row slots are live; some device is full in every draw.
All inputs are finite; a program needn't handle non-finite values.
Results may differ from the reference program's by a relative error of at most 0.001.
The reference program's roundings to bfloat16 on the way (of `old_weights` and `local`) count: a program that leaves them out, or rounds other values in their place, can miss the bound.
Values may be sent and summed in bfloat16 or wider, within the bound.
A program may use at most 64 MiB of HBM per device.

```python
import math
import jax
import jax.numpy as jnp
from jax import lax

D = 2048
HID = 256
MICRO = 4
ROW_MB = 64
ROWS = 256
EXPERTS = 4
N_DP = 2
N_PLACE = 16


def slot_draw(key, count):
    keys = jax.random.split(key, 4)
    first = jax.random.randint(keys[0], (count - EXPERTS,), 0, EXPERTS)
    second = jax.random.randint(keys[1], (count - EXPERTS,), 0, EXPERTS)
    extra = jnp.minimum(first, second)
    labels = jax.random.permutation(keys[2], EXPERTS)
    slots = labels[jnp.concatenate([jnp.arange(EXPERTS, dtype=jnp.int32), extra.astype(jnp.int32)])]
    return jax.random.permutation(keys[3], slots).astype(jnp.int32)


def draw_old_slots(key, part):
    return slot_draw(jax.random.fold_in(key, 11), N_PLACE)


def draw_new_slots(key, part):
    return slot_draw(jax.random.fold_in(key, 23), N_PLACE)


def draw_row_count(key, part):
    keys = jax.random.split(jax.random.fold_in(key, 37), 2)
    counts = jax.random.randint(keys[0], (N_DP * N_PLACE,), 1, ROWS + 1)
    spot = jax.random.randint(keys[1], (), 0, N_DP * N_PLACE)
    filled = jnp.where(jnp.arange(N_DP * N_PLACE) == spot, ROWS, counts)
    return filled.reshape(N_DP, N_PLACE).astype(jnp.int32)


def shard_levels(key, shape, cuts, least, top_value):
    factor_of, own = 1.0, jax.random.fold_in(key, 6)
    for dim, parts in cuts:
        steps = jnp.exp(jax.random.uniform(jax.random.fold_in(own, dim), (parts,), jnp.float32, least / len(cuts), top_value / len(cuts)))
        factor_of = factor_of * jnp.repeat(steps, shape[dim] // parts).reshape([-1 if axis == dim else 1 for axis in range(len(shape))])
    return factor_of


def noise(rng, extent, scale, limit, cuts=(), kind=jnp.bfloat16):
    entries = scale * jax.random.normal(rng, extent, jnp.float32)
    if cuts:
        entries = entries * shard_levels(rng, extent, cuts, -0.22, 0.18)
    return jnp.clip(entries, -limit, limit).astype(kind)


def setup_inputs(seed: int = 0) -> dict:
    seeds = jax.random.split(jax.random.key(seed), 10)
    return {
        "tokens": noise(seeds[0], (N_DP, N_PLACE, ROWS, D), 1.0, 6.0, ((0, 2), (1, 16))),
        "hidden_grad": noise(seeds[1], (N_DP, N_PLACE, ROWS, HID), 1.0, 6.0, ((0, 2), (1, 16))),
        "routing": jax.vmap(lambda own: jax.random.permutation(own, ROW_MB))(jax.random.split(seeds[2], N_DP * N_PLACE * MICRO)).reshape((N_DP, N_PLACE, MICRO, ROW_MB)).astype(jnp.int32),
        "row_count": draw_row_count(jax.random.fold_in(seeds[9], 71), 0),
        "old_slots": draw_old_slots(jax.random.fold_in(seeds[9], 71), 0),
        "new_slots": draw_new_slots(jax.random.fold_in(seeds[9], 71), 0),
        "master": noise(seeds[6], (EXPERTS, D, 2 * HID), D ** -0.5, 0.125, ((1, 32),), jnp.float32),
        "first_moment": noise(seeds[7], (EXPERTS, D, 2 * HID), 0.003, 0.018, ((1, 32),), jnp.float32),
        "second_moment": jnp.clip(jnp.exp(math.log(0.0001) - 4.6051702 * jax.random.uniform(seeds[8], (EXPERTS, D, 2 * HID), jnp.float32) ** shard_levels(seeds[8], (EXPERTS, D, 2 * HID), ((1, 32),), -0.2, 0.2)), 9.999999974752427e-07, 0.0001),
    }


decay_first = 0.9
decay_second = 0.95
learn_rate = 0.001
weight_decay = 0.1
epsilon = 1e-08
step_number = 20.0

def device_grad(rows_in, grads_in, order, count, weights):
    width = weights.shape[1]
    half = width // 2
    total = jnp.zeros((rows_in.shape[1], width), jnp.float32)
    wide = weights.astype(jnp.float32)
    for batch_index in range(MICRO):
        start = batch_index * ROW_MB
        picked = jnp.take(rows_in, start + order[batch_index].astype(jnp.int32), axis=0)
        picked_wide = picked.astype(jnp.float32)
        both = jnp.dot(picked_wide, wide, precision=lax.Precision.HIGHEST)
        gate = both[:, :half]
        upward = both[:, half:]
        sigma = jax.nn.sigmoid(gate)
        active = gate * sigma
        slope = sigma * (1.0 + gate * (1.0 - sigma))
        live = start + jnp.arange(ROW_MB, dtype=jnp.int32) < count
        incoming = jnp.where(live[:, None], grads_in[start:start + ROW_MB].astype(jnp.float32), 0.0)
        local = jnp.concatenate([incoming * upward * slope, incoming * active], axis=1).astype(jnp.bfloat16)
        total = total + jnp.dot(picked_wide.T, local.astype(jnp.float32), precision=lax.Precision.HIGHEST)
    return total

def reference(tokens, hidden_grad, routing, row_count, old_slots, new_slots, master, first_moment, second_moment):
    devices = N_DP * N_PLACE
    old_weights = master.astype(jnp.bfloat16)
    flat_tokens = tokens.reshape(devices, ROWS, D)
    flat_grads = hidden_grad.reshape(devices, ROWS, HID)
    flat_order = routing.reshape(devices, MICRO, ROW_MB)
    flat_count = row_count.reshape(devices)
    flat_slot = jnp.tile(old_slots, N_DP)

    def visit(summed, item):
        rows_in, grads_in, order, count, slot = item
        weights = old_weights[slot]
        grad = device_grad(rows_in, grads_in, order, count, weights)
        return (summed.at[slot].add(grad), None)
    start_sum = jnp.zeros((EXPERTS, D, 2 * HID), jnp.float32)
    summed, _ = lax.scan(visit, start_sum, (flat_tokens, flat_grads, flat_order, flat_count, flat_slot))
    select = (old_slots[:, None] == jnp.arange(EXPERTS, dtype=jnp.int32)[None, :]).astype(jnp.float32)
    per_slot = lax.optimization_barrier(jnp.sum(row_count.astype(jnp.float32), axis=0))
    total = jnp.dot(per_slot, select, precision=lax.Precision.HIGHEST)
    grad = summed / total[:, None, None]
    new_first = decay_first * first_moment + (1.0 - decay_first) * grad
    new_second = decay_second * second_moment + (1.0 - decay_second) * grad * grad
    first_hat = new_first / (1.0 - decay_first ** step_number)
    second_hat = new_second / (1.0 - decay_second ** step_number)
    new_master = master - learn_rate * (first_hat / (jnp.sqrt(second_hat) + epsilon) + weight_decay * master)
    new_weights = new_master.astype(jnp.bfloat16)[new_slots]
    return (new_weights, new_master, new_first, new_second)
```

```python
import jax
import jax.numpy as jnp
from jax import lax
from jax.sharding import PartitionSpec as P

decay_first = 0.9
decay_second = 0.95
learn_rate = 0.001
weight_decay = 0.1
epsilon = 1e-08
step_number = 20.0


def spread(shard, slots):
    experts, rows_shard, width = shard.shape
    places = lax.axis_size("place")
    select = (slots[:, None] == jnp.arange(experts, dtype=jnp.int32)[None, :]).astype(jnp.bfloat16)
    picked = jnp.dot(
        select, shard.reshape(experts, rows_shard * width), preferred_element_type=jnp.float32
    ).astype(jnp.bfloat16)
    landed = lax.all_to_all(
        picked.reshape(places, rows_shard, width), "place", split_axis=0, concat_axis=0, tiled=True
    )
    whole = lax.all_gather(landed.reshape(places * rows_shard, width), "dp", axis=0, tiled=True)
    return whole


def batch_grad(total, rows_in, grads_in, order, count, weights, start):
    rows = order.shape[0]
    half = weights.shape[1] // 2
    picked = jnp.take(rows_in, start + order, axis=0)
    both = jnp.dot(picked, weights, preferred_element_type=jnp.float32)
    gate = both[:, :half]
    upward = both[:, half:]
    sigma = jax.nn.sigmoid(gate)
    active = gate * sigma
    slope = sigma * (1.0 + gate * (1.0 - sigma))
    live = start + jnp.arange(rows, dtype=jnp.int32) < count
    incoming = jnp.where(live[:, None], grads_in[start : start + rows].astype(jnp.float32), 0.0)
    local = jnp.concatenate([incoming * upward * slope, incoming * active], axis=1).astype(
        jnp.bfloat16
    )
    return total + lax.dot_general(
        picked, local, (((0,), (0,)), ((), ())), preferred_element_type=jnp.float32
    )


def shards(
    tokens,
    hidden_grad,
    routing,
    row_count,
    old_slots,
    new_slots,
    master,
    first_moment,
    second_moment,
):
    places = lax.axis_size("place")
    groups = lax.axis_size("dp")
    experts, rows_shard, width = master.shape
    place_here = lax.axis_index("place")
    group_here = lax.axis_index("dp")
    weights = spread(master.astype(jnp.bfloat16), old_slots)
    rows_in = tokens[0, 0]
    grads_in = hidden_grad[0, 0]
    order = routing[0, 0]
    count = row_count[group_here, place_here]
    batch_rows = order.shape[1]
    summed = jnp.zeros((rows_in.shape[1], width), jnp.float32)
    for batch_index in range(order.shape[0]):
        start = batch_index * batch_rows
        summed = batch_grad(summed, rows_in, grads_in, order[batch_index], count, weights, start)
    select = (old_slots[:, None] == jnp.arange(experts, dtype=jnp.int32)[None, :]).astype(
        jnp.float32
    )
    blocks = summed.reshape(groups, places, rows_shard, width)
    landed = lax.all_to_all(blocks, "place", split_axis=1, concat_axis=1, tiled=True)
    merged = jnp.einsum(
        "se,dsx->dex",
        select,
        landed.reshape(groups, places, rows_shard * width),
        precision=lax.Precision.HIGHEST,
    )
    mine = lax.psum_scatter(merged, "dp", scatter_dimension=0, tiled=True)
    grad_sum = mine.reshape(experts, rows_shard, width)
    per_slot = jnp.sum(row_count.astype(jnp.float32), axis=0)
    total = jnp.dot(per_slot, select, precision=lax.Precision.HIGHEST)
    grad = grad_sum / total[:, None, None]
    new_first = decay_first * first_moment + (1.0 - decay_first) * grad
    new_second = decay_second * second_moment + (1.0 - decay_second) * grad * grad
    first_hat = new_first / (1.0 - decay_first**step_number)
    second_hat = new_second / (1.0 - decay_second**step_number)
    new_master = master - learn_rate * (
        first_hat / (jnp.sqrt(second_hat) + epsilon) + weight_decay * master
    )
    new_weights = spread(new_master.astype(jnp.bfloat16), new_slots)
    return (new_weights[None], new_master, new_first, new_second)


def whole_gather(shard):
    return lax.all_gather(shard, ("dp", "place"), axis=0, tiled=False)


def adam(grad, master, first_moment, second_moment):
    new_first = decay_first * first_moment + (1.0 - decay_first) * grad
    new_second = decay_second * second_moment + (1.0 - decay_second) * grad * grad
    first_hat = new_first / (1.0 - decay_first**step_number)
    second_hat = new_second / (1.0 - decay_second**step_number)
    new_master = master - learn_rate * (
        first_hat / (jnp.sqrt(second_hat) + epsilon) + weight_decay * master
    )
    return new_master, new_first, new_second


def gathered(
    tokens,
    hidden_grad,
    routing,
    row_count,
    old_slots,
    new_slots,
    master,
    first_moment,
    second_moment,
):
    places = lax.axis_size("place")
    groups = lax.axis_size("dp")
    devices = places * groups
    experts, rows_shard, width = master.shape
    half = width // 2
    place_here = lax.axis_index("place")
    group_here = lax.axis_index("dp")
    rows_in = tokens[0, 0]
    rows, depth = rows_in.shape
    order = routing[0, 0]
    batches, batch_rows = order.shape
    turned = rows_in.T.reshape(devices, rows_shard, rows)
    all_weights = whole_gather(master.astype(jnp.bfloat16))
    columns = lax.all_to_all(turned, ("dp", "place"), split_axis=0, concat_axis=0, tiled=True)
    weights = lax.dynamic_index_in_dim(
        all_weights, old_slots[place_here], axis=1, keepdims=False
    ).reshape(depth, width)
    live = jnp.arange(rows, dtype=jnp.int32) < row_count[group_here, place_here]
    place_of = (
        order[:, None, :] == jnp.arange(batch_rows, dtype=jnp.int32)[None, :, None]
    ) & live.reshape(batches, 1, batch_rows)
    incoming = jnp.einsum(
        "mri,mik->mrk",
        place_of.astype(jnp.bfloat16),
        hidden_grad[0, 0].reshape(batches, batch_rows, half),
        preferred_element_type=jnp.float32,
    ).reshape(rows, half)
    both = jnp.dot(rows_in, weights, preferred_element_type=jnp.float32)
    gate = both[:, :half]
    upward = both[:, half:]
    sigma = jax.nn.sigmoid(gate)
    active = gate * sigma
    slope = sigma * (1.0 + gate * (1.0 - sigma))
    local = jnp.concatenate([incoming * upward * slope, incoming * active], axis=1).astype(
        jnp.bfloat16
    )
    all_local = whole_gather(local)
    select = old_slots[None, :] == jnp.arange(experts, dtype=jnp.int32)[:, None]
    chosen = jnp.tile(select, (1, groups))
    stacked = jnp.where(
        chosen[:, None, :, None], columns.transpose(1, 0, 2)[None], jnp.bfloat16(0)
    ).reshape(experts * rows_shard, devices * rows)
    grad_sum = jnp.dot(
        stacked, all_local.reshape(devices * rows, width), preferred_element_type=jnp.float32
    ).reshape(experts, rows_shard, width)
    per_slot = jnp.sum(row_count.astype(jnp.float32), axis=0)
    total = jnp.sum(jnp.where(select, per_slot[None, :], 0.0), axis=1)
    grad = grad_sum / total[:, None, None]
    new_master, new_first, new_second = adam(grad, master, first_moment, second_moment)
    all_new = whole_gather(new_master.astype(jnp.bfloat16))
    new_weights = lax.dynamic_index_in_dim(all_new, new_slots[place_here], axis=1, keepdims=True)
    return (
        new_weights.reshape(1, depth, width),
        new_master,
        new_first,
        new_second,
    )


def fits(mesh):
    return mesh.size <= 64


def solution(mesh):
    placed = (
        P("dp", "place", None, None),
        P("dp", "place", None, None),
        P("dp", "place", None, None),
        P(),
        P(),
        P(),
        P(None, ("dp", "place"), None),
        P(None, ("dp", "place"), None),
        P(None, ("dp", "place"), None),
    )
    return jax.shard_map(
        gathered if fits(mesh) else shards,
        mesh=mesh,
        in_specs=placed,
        out_specs=(
            P("place", None, None),
            P(None, ("dp", "place"), None),
            P(None, ("dp", "place"), None),
            P(None, ("dp", "place"), None),
        ),
        check_vma=False,
    )
```

```python
import functools

import jax
import jax.numpy as jnp
from jax import lax
from jax.experimental import pallas as pl
from jax.experimental.pallas import tpu as pltpu
from jax.sharding import PartitionSpec as P

decay_first = 0.9
decay_second = 0.95
learn_rate = 0.001
weight_decay = 0.1
epsilon = 1e-08
step_number = 20.0


def spread(shard, slots):
    experts, rows_shard, width = shard.shape
    places = lax.axis_size("place")
    select = (slots[:, None] == jnp.arange(experts, dtype=jnp.int32)[None, :]).astype(jnp.bfloat16)
    picked = jnp.dot(
        select, shard.reshape(experts, rows_shard * width), preferred_element_type=jnp.float32
    ).astype(jnp.bfloat16)
    landed = lax.all_to_all(
        picked.reshape(places, rows_shard, width), "place", split_axis=0, concat_axis=0, tiled=True
    )
    whole = lax.all_gather(landed.reshape(places * rows_shard, width), "dp", axis=0, tiled=True)
    return whole


def batch_grad(total, rows_in, grads_in, order, count, weights, start):
    rows = order.shape[0]
    half = weights.shape[1] // 2
    picked = jnp.take(rows_in, start + order, axis=0)
    both = jnp.dot(picked, weights, preferred_element_type=jnp.float32)
    gate = both[:, :half]
    upward = both[:, half:]
    sigma = jax.nn.sigmoid(gate)
    active = gate * sigma
    slope = sigma * (1.0 + gate * (1.0 - sigma))
    live = start + jnp.arange(rows, dtype=jnp.int32) < count
    incoming = jnp.where(live[:, None], grads_in[start : start + rows].astype(jnp.float32), 0.0)
    local = jnp.concatenate([incoming * upward * slope, incoming * active], axis=1).astype(
        jnp.bfloat16
    )
    return total + lax.dot_general(
        picked, local, (((0,), (0,)), ((), ())), preferred_element_type=jnp.float32
    )


def shards(
    tokens,
    hidden_grad,
    routing,
    row_count,
    old_slots,
    new_slots,
    master,
    first_moment,
    second_moment,
):
    places = lax.axis_size("place")
    groups = lax.axis_size("dp")
    experts, rows_shard, width = master.shape
    place_here = lax.axis_index("place")
    group_here = lax.axis_index("dp")
    weights = spread(master.astype(jnp.bfloat16), old_slots)
    rows_in = tokens[0, 0]
    grads_in = hidden_grad[0, 0]
    order = routing[0, 0]
    count = row_count[group_here, place_here]
    batch_rows = order.shape[1]
    summed = jnp.zeros((rows_in.shape[1], width), jnp.float32)
    for batch_index in range(order.shape[0]):
        start = batch_index * batch_rows
        summed = batch_grad(summed, rows_in, grads_in, order[batch_index], count, weights, start)
    select = (old_slots[:, None] == jnp.arange(experts, dtype=jnp.int32)[None, :]).astype(
        jnp.float32
    )
    blocks = summed.reshape(groups, places, rows_shard, width)
    landed = lax.all_to_all(blocks, "place", split_axis=1, concat_axis=1, tiled=True)
    merged = jnp.einsum(
        "se,dsx->dex",
        select,
        landed.reshape(groups, places, rows_shard * width),
        precision=lax.Precision.HIGHEST,
    )
    mine = lax.psum_scatter(merged, "dp", scatter_dimension=0, tiled=True)
    grad_sum = mine.reshape(experts, rows_shard, width)
    per_slot = jnp.sum(row_count.astype(jnp.float32), axis=0)
    total = jnp.dot(per_slot, select, precision=lax.Precision.HIGHEST)
    grad = grad_sum / total[:, None, None]
    new_first = decay_first * first_moment + (1.0 - decay_first) * grad
    new_second = decay_second * second_moment + (1.0 - decay_second) * grad * grad
    first_hat = new_first / (1.0 - decay_first**step_number)
    second_hat = new_second / (1.0 - decay_second**step_number)
    new_master = master - learn_rate * (
        first_hat / (jnp.sqrt(second_hat) + epsilon) + weight_decay * master
    )
    new_weights = spread(new_master.astype(jnp.bfloat16), new_slots)
    return (new_weights[None], new_master, new_first, new_second)


MESH = pl.DeviceIdType.MESH


def route(groups, places):
    here = lax.axis_index("place")
    return lax.axis_index("dp"), here // 4, (here // 2) % 2, here % 2


def gather_kernel(groups, places, own_ref, all_ref, send_sem, recv_sem, own_sem):
    levels = places // 4
    y, z, x, c = route(groups, places)

    def block(y, z, x, c):
        return y * places + z * 4 + x * 2 + c

    def device(y, z, x, c):
        return (y, z * 4 + x * 2 + c)

    x_first, y_first = (x + 1 - c) % 2, (y + c) % 2
    x_last, y_last = (x + c) % 2, (y + 1 - c) % 2
    lines = [device(y, (z + k) % levels, x, c) for k in range(1, levels)]
    first = device(y_first, z, x_first, c)
    last = device(y_last, z, x_last, c)
    sibling = device(y, z, x, 1 - c)
    partners = lines + [first, last, sibling]

    barrier = pltpu.get_barrier_semaphore()
    for partner in partners:
        pl.semaphore_signal(barrier, inc=1, device_id=partner, device_id_type=MESH)
    pl.semaphore_wait(barrier, len(partners))

    mine = block(y, z, x, c)
    sends = []

    def send(index, partner, source=None):
        copy = pltpu.make_async_remote_copy(
            src_ref=all_ref.at[index] if source is None else source,
            dst_ref=all_ref.at[index],
            send_sem=send_sem.at[len(sends)],
            recv_sem=recv_sem.at[index],
            device_id=partner,
            device_id_type=MESH,
        )
        copy.start()
        sends.append(copy)

    def arrived(index):
        pltpu.make_async_remote_copy(
            src_ref=all_ref.at[index],
            dst_ref=all_ref.at[index],
            send_sem=send_sem.at[0],
            recv_sem=recv_sem.at[index],
            device_id=sibling,
            device_id_type=MESH,
        ).wait_recv()

    for partner in (first, last, *lines, sibling):
        send(mine, partner, own_ref)
    keep = pltpu.make_async_copy(own_ref, all_ref.at[mine], own_sem)
    keep.start()
    for k in range(levels):
        level = (z + k) % levels
        if k:
            straight = block(y, level, x, c)
            arrived(straight)
            for partner in (first, last, sibling):
                send(straight, partner)
        over = block(y_first, level, x_first, c)
        arrived(over)
        for partner in (last, sibling):
            send(over, partner)
    for k in range(levels):
        level = (z + k) % levels
        for index in (block(y_last, level, x_last, c), block(1 - y, level, 1 - x, c)):
            arrived(index)
            send(index, sibling)
    for k in range(levels):
        level = (z + k) % levels
        for side in range(2):
            for group in range(2):
                arrived(block(group, level, side, 1 - c))
    keep.wait()
    for copy in sends:
        copy.wait_send()


def whole_gather(shard):
    places = lax.axis_size("place")
    groups = lax.axis_size("dp")
    devices = groups * places
    return pl.pallas_call(
        functools.partial(gather_kernel, groups, places),
        out_shape=jax.ShapeDtypeStruct((devices,) + shard.shape, shard.dtype),
        in_specs=[pl.BlockSpec(memory_space=pl.ANY)],
        out_specs=pl.BlockSpec(memory_space=pl.ANY),
        scratch_shapes=[
            pltpu.SemaphoreType.DMA((devices,)),
            pltpu.SemaphoreType.DMA((devices,)),
            pltpu.SemaphoreType.DMA,
        ],
        compiler_params=pltpu.CompilerParams(collective_id=0, has_side_effects=True),
    )(shard)


def adam(grad, master, first_moment, second_moment):
    new_first = decay_first * first_moment + (1.0 - decay_first) * grad
    new_second = decay_second * second_moment + (1.0 - decay_second) * grad * grad
    first_hat = new_first / (1.0 - decay_first**step_number)
    second_hat = new_second / (1.0 - decay_second**step_number)
    new_master = master - learn_rate * (
        first_hat / (jnp.sqrt(second_hat) + epsilon) + weight_decay * master
    )
    return new_master, new_first, new_second


def gathered(
    tokens,
    hidden_grad,
    routing,
    row_count,
    old_slots,
    new_slots,
    master,
    first_moment,
    second_moment,
):
    places = lax.axis_size("place")
    groups = lax.axis_size("dp")
    devices = places * groups
    experts, rows_shard, width = master.shape
    half = width // 2
    place_here = lax.axis_index("place")
    group_here = lax.axis_index("dp")
    rows_in = tokens[0, 0]
    rows, depth = rows_in.shape
    order = routing[0, 0]
    batches, batch_rows = order.shape
    turned = rows_in.T.reshape(devices, rows_shard, rows)
    all_weights = whole_gather(master.astype(jnp.bfloat16))
    columns = lax.all_to_all(turned, ("dp", "place"), split_axis=0, concat_axis=0, tiled=True)
    weights = lax.dynamic_index_in_dim(
        all_weights, old_slots[place_here], axis=1, keepdims=False
    ).reshape(depth, width)
    live = jnp.arange(rows, dtype=jnp.int32) < row_count[group_here, place_here]
    place_of = (
        order[:, None, :] == jnp.arange(batch_rows, dtype=jnp.int32)[None, :, None]
    ) & live.reshape(batches, 1, batch_rows)
    incoming = jnp.einsum(
        "mri,mik->mrk",
        place_of.astype(jnp.bfloat16),
        hidden_grad[0, 0].reshape(batches, batch_rows, half),
        preferred_element_type=jnp.float32,
    ).reshape(rows, half)
    both = jnp.dot(rows_in, weights, preferred_element_type=jnp.float32)
    gate = both[:, :half]
    upward = both[:, half:]
    sigma = jax.nn.sigmoid(gate)
    active = gate * sigma
    slope = sigma * (1.0 + gate * (1.0 - sigma))
    local = jnp.concatenate([incoming * upward * slope, incoming * active], axis=1).astype(
        jnp.bfloat16
    )
    all_local = whole_gather(local.reshape(experts, rows * width // (experts * width), width))
    select = old_slots[None, :] == jnp.arange(experts, dtype=jnp.int32)[:, None]
    chosen = jnp.tile(select, (1, groups))
    stacked = jnp.where(
        chosen[:, None, :, None], columns.transpose(1, 0, 2)[None], jnp.bfloat16(0)
    ).reshape(experts * rows_shard, devices * rows)
    grad_sum = jnp.dot(
        stacked, all_local.reshape(devices * rows, width), preferred_element_type=jnp.float32
    ).reshape(experts, rows_shard, width)
    per_slot = jnp.sum(row_count.astype(jnp.float32), axis=0)
    total = jnp.sum(jnp.where(select, per_slot[None, :], 0.0), axis=1)
    grad = grad_sum / total[:, None, None]
    new_master, new_first, new_second = adam(grad, master, first_moment, second_moment)
    all_new = whole_gather(new_master.astype(jnp.bfloat16))
    new_weights = lax.dynamic_index_in_dim(all_new, new_slots[place_here], axis=1, keepdims=True)
    return (
        new_weights.reshape(1, depth, width),
        new_master,
        new_first,
        new_second,
    )


def fits(mesh):
    return mesh.shape["dp"] == 2 and mesh.shape["place"] in (4, 8, 16)


def solution(mesh):
    placed = (
        P("dp", "place", None, None),
        P("dp", "place", None, None),
        P("dp", "place", None, None),
        P(),
        P(),
        P(),
        P(None, ("dp", "place"), None),
        P(None, ("dp", "place"), None),
        P(None, ("dp", "place"), None),
    )
    return jax.shard_map(
        gathered if fits(mesh) else shards,
        mesh=mesh,
        in_specs=placed,
        out_specs=(
            P("place", None, None),
            P(None, ("dp", "place"), None),
            P(None, ("dp", "place"), None),
            P(None, ("dp", "place"), None),
        ),
        check_vma=False,
    )
```

```python
import functools

import jax
import jax.numpy as jnp
from jax import lax
from jax.experimental import pallas as pl
from jax.experimental.pallas import tpu as pltpu
from jax.sharding import PartitionSpec as P

decay_first = 0.9
decay_second = 0.95
learn_rate = 0.001
weight_decay = 0.1
epsilon = 1e-08
step_number = 20.0


def spread(shard, slots):
    experts, rows_shard, width = shard.shape
    places = lax.axis_size("place")
    select = (slots[:, None] == jnp.arange(experts, dtype=jnp.int32)[None, :]).astype(jnp.bfloat16)
    picked = jnp.dot(
        select, shard.reshape(experts, rows_shard * width), preferred_element_type=jnp.float32
    ).astype(jnp.bfloat16)
    landed = lax.all_to_all(
        picked.reshape(places, rows_shard, width), "place", split_axis=0, concat_axis=0, tiled=True
    )
    whole = lax.all_gather(landed.reshape(places * rows_shard, width), "dp", axis=0, tiled=True)
    return whole


def batch_grad(total, rows_in, grads_in, order, count, weights, start):
    rows = order.shape[0]
    half = weights.shape[1] // 2
    picked = jnp.take(rows_in, start + order, axis=0)
    both = jnp.dot(picked, weights, preferred_element_type=jnp.float32)
    gate = both[:, :half]
    upward = both[:, half:]
    sigma = jax.nn.sigmoid(gate)
    active = gate * sigma
    slope = sigma * (1.0 + gate * (1.0 - sigma))
    live = start + jnp.arange(rows, dtype=jnp.int32) < count
    incoming = jnp.where(live[:, None], grads_in[start : start + rows].astype(jnp.float32), 0.0)
    local = jnp.concatenate([incoming * upward * slope, incoming * active], axis=1).astype(
        jnp.bfloat16
    )
    return total + lax.dot_general(
        picked, local, (((0,), (0,)), ((), ())), preferred_element_type=jnp.float32
    )


def shards(
    tokens,
    hidden_grad,
    routing,
    row_count,
    old_slots,
    new_slots,
    master,
    first_moment,
    second_moment,
):
    places = lax.axis_size("place")
    groups = lax.axis_size("dp")
    experts, rows_shard, width = master.shape
    place_here = lax.axis_index("place")
    group_here = lax.axis_index("dp")
    weights = spread(master.astype(jnp.bfloat16), old_slots)
    rows_in = tokens[0, 0]
    grads_in = hidden_grad[0, 0]
    order = routing[0, 0]
    count = row_count[group_here, place_here]
    batch_rows = order.shape[1]
    summed = jnp.zeros((rows_in.shape[1], width), jnp.float32)
    for batch_index in range(order.shape[0]):
        start = batch_index * batch_rows
        summed = batch_grad(summed, rows_in, grads_in, order[batch_index], count, weights, start)
    select = (old_slots[:, None] == jnp.arange(experts, dtype=jnp.int32)[None, :]).astype(
        jnp.float32
    )
    blocks = summed.reshape(groups, places, rows_shard, width)
    landed = lax.all_to_all(blocks, "place", split_axis=1, concat_axis=1, tiled=True)
    merged = jnp.einsum(
        "se,dsx->dex",
        select,
        landed.reshape(groups, places, rows_shard * width),
        precision=lax.Precision.HIGHEST,
    )
    mine = lax.psum_scatter(merged, "dp", scatter_dimension=0, tiled=True)
    grad_sum = mine.reshape(experts, rows_shard, width)
    per_slot = jnp.sum(row_count.astype(jnp.float32), axis=0)
    total = jnp.dot(per_slot, select, precision=lax.Precision.HIGHEST)
    grad = grad_sum / total[:, None, None]
    new_first = decay_first * first_moment + (1.0 - decay_first) * grad
    new_second = decay_second * second_moment + (1.0 - decay_second) * grad * grad
    first_hat = new_first / (1.0 - decay_first**step_number)
    second_hat = new_second / (1.0 - decay_second**step_number)
    new_master = master - learn_rate * (
        first_hat / (jnp.sqrt(second_hat) + epsilon) + weight_decay * master
    )
    new_weights = spread(new_master.astype(jnp.bfloat16), new_slots)
    return (new_weights[None], new_master, new_first, new_second)


MESH = pl.DeviceIdType.MESH


def spot(places):
    here = lax.axis_index("place")
    return lax.axis_index("dp"), here // 4, (here // 2) % 2, here % 2


def device(y, z, x, c):
    return (y, z * 4 + x * 2 + c)


def meet(partners, z, levels, up, down):
    barrier = pltpu.get_barrier_semaphore()

    def greet(partner):
        pl.semaphore_signal(barrier, inc=1, device_id=partner, device_id_type=MESH)

    for partner in partners:
        greet(partner)
    pl.when(z < levels - 1)(lambda: greet(up))
    pl.when(z > 0)(lambda: greet(down))
    has_down = (z + levels - 2) // (levels - 1)
    has_up = (2 * levels - 3 - z) // (levels - 1)
    pl.semaphore_wait(barrier, len(partners) + has_up + has_down)


def remote(source, target, send_sem, recv_sem, partner):
    return pltpu.make_async_remote_copy(
        src_ref=source,
        dst_ref=target,
        send_sem=send_sem,
        recv_sem=recv_sem,
        device_id=partner,
        device_id_type=MESH,
    )


def gather_kernel(places, own_ref, all_ref, send_sem, recv_sem, own_sem):
    levels = places // 4
    y, z, x, c = spot(places)

    def block(y, z, x, c):
        return y * places + z * 4 + x * 2 + c

    x_first, y_first = (x + 1 - c) % 2, (y + c) % 2
    x_last, y_last = (x + c) % 2, (y + 1 - c) % 2
    up, down = device(y, z + 1, x, c), device(y, z - 1, x, c)
    first = device(y_first, z, x_first, c)
    last = device(y_last, z, x_last, c)
    sibling = device(y, z, x, 1 - c)
    meet([first, last, sibling], z, levels, up, down)

    def copy(kind, level, index, partner, source=None):
        return remote(
            all_ref.at[index] if source is None else source,
            all_ref.at[index],
            send_sem.at[kind, level],
            recv_sem.at[index],
            partner,
        )

    def arrived(index):
        copy(0, 0, index, sibling).wait_recv()

    mine = block(y, z, x, c)
    pl.when(z < levels - 1)(lambda: copy(0, z, mine, up, own_ref).start())
    pl.when(z > 0)(lambda: copy(1, z, mine, down, own_ref).start())
    copy(2, z, mine, first, own_ref).start()
    copy(3, z, mine, last, own_ref).start()
    copy(4, z, mine, sibling, own_ref).start()
    keep = pltpu.make_async_copy(own_ref, all_ref.at[mine], own_sem)
    keep.start()

    def straight(level, below):
        index = block(y, level, x, c)
        arrived(index)
        if below:
            pl.when(z < levels - 1)(lambda: copy(0, level, index, up).start())
        else:
            pl.when(z > 0)(lambda: copy(1, level, index, down).start())
        copy(2, level, index, first).start()
        copy(3, level, index, last).start()
        copy(4, level, index, sibling).start()

    def over(level, below):
        index = block(y_first, level, x_first, c)
        arrived(index)
        copy(5, level, index, last).start()
        copy(6, level, index, sibling).start()

    def both_ways(k, visit):
        if k == 0:
            visit(z, True)
        else:
            pl.when(z >= k)(lambda: visit(z - k, True))
            pl.when(z < levels - k)(lambda: visit(z + k, False))

    for k in range(1, levels):
        both_ways(k, straight)
        both_ways(k - 1, over)
    both_ways(levels - 1, over)

    def ending(level, below):
        for kind, index in ((7, block(y_last, level, x_last, c)), (8, block(1 - y, level, 1 - x, c))):
            arrived(index)
            copy(kind, level, index, sibling).start()

    for k in range(levels):
        both_ways(k, ending)
    for level in range(levels):
        for side in range(2):
            for group in range(2):
                arrived(block(group, level, side, 1 - c))
    keep.wait()
    for level in range(levels):
        for kind in range(2, 9):
            copy(kind, level, mine, sibling).wait_send()
        pl.when((z >= level) & (z < levels - 1))(
            lambda level=level: copy(0, level, mine, sibling).wait_send()
        )
        pl.when((z <= level) & (z > 0))(
            lambda level=level: copy(1, level, mine, sibling).wait_send()
        )


def whole_gather(shard):
    places = lax.axis_size("place")
    devices = lax.axis_size("dp") * places
    levels = places // 4
    return pl.pallas_call(
        functools.partial(gather_kernel, places),
        out_shape=jax.ShapeDtypeStruct((devices,) + shard.shape, shard.dtype),
        in_specs=[pl.BlockSpec(memory_space=pl.ANY)],
        out_specs=pl.BlockSpec(memory_space=pl.ANY),
        scratch_shapes=[
            pltpu.SemaphoreType.DMA((9, levels)),
            pltpu.SemaphoreType.DMA((devices,)),
            pltpu.SemaphoreType.DMA,
        ],
        compiler_params=pltpu.CompilerParams(collective_id=0, has_side_effects=True),
    )(shard)


def expert_kernel(
    places, slots_ref, own_ref, out_ref, line, held, picked, line_send, line_recv, send_sem, recv_sem
):
    levels = places // 4
    y, z, x, c = spot(places)
    up, down = device(y, z + 1, x, c), device(y, z - 1, x, c)
    shifts = [(0, 1, 0), (1, 0, 0), (0, 1, 1), (1, 0, 1), (1, 1, 0), (1, 1, 1), (0, 0, 1)]
    plane = [((y + dy) % 2, (x + dx) % 2, (c + dc) % 2) for dy, dx, dc in shifts]
    partners = [device(there_y, z, there_x, there_c) for there_y, there_x, there_c in plane]
    line[z] = own_ref[...]
    meet(partners, z, levels, up, down)

    def pass_on(way, level):
        return remote(
            line.at[level],
            line.at[level],
            line_send.at[way, level],
            line_recv.at[level],
            (up, down)[way],
        )

    def hand(j, level, index):
        return remote(
            picked.at[j, level],
            out_ref.at[index],
            send_sem.at[j, level],
            recv_sem.at[index],
            partners[j],
        )

    def fan(level):
        index = y * places + level * 4 + x * 2 + c
        held[...] = line[level]
        for j, partner in enumerate(partners):
            picked[j, level] = held[slots_ref[partner[1]]]
            hand(j, level, index).start()
        out_ref[index] = held[slots_ref[z * 4 + x * 2 + c]]

    pl.when(z < levels - 1)(lambda: pass_on(0, z).start())
    pl.when(z > 0)(lambda: pass_on(1, z).start())
    fan(z)

    def below(level):
        pass_on(0, level).wait_recv()
        pl.when(z < levels - 1)(lambda: pass_on(0, level).start())
        fan(level)

    def above(level):
        pass_on(1, level).wait_recv()
        pl.when(z > 0)(lambda: pass_on(1, level).start())
        fan(level)

    for k in range(1, levels):
        pl.when(z >= k)(lambda k=k: below(z - k))
        pl.when(z < levels - k)(lambda k=k: above(z + k))
    for level in range(levels):
        for j, (there_y, there_x, there_c) in enumerate(plane):
            hand(j, level, there_y * places + level * 4 + there_x * 2 + there_c).wait()
        pl.when((z >= level) & (z < levels - 1))(lambda level=level: pass_on(0, level).wait_send())
        pl.when((z <= level) & (z > 0))(lambda level=level: pass_on(1, level).wait_send())


def expert_rows(shard, slots):
    places = lax.axis_size("place")
    devices = lax.axis_size("dp") * places
    levels = places // 4
    tile = shard.shape[1:]
    return pl.pallas_call(
        functools.partial(expert_kernel, places),
        out_shape=jax.ShapeDtypeStruct((devices,) + tile, shard.dtype),
        in_specs=[
            pl.BlockSpec(memory_space=pltpu.SMEM),
            pl.BlockSpec(memory_space=pltpu.VMEM),
        ],
        out_specs=pl.BlockSpec(memory_space=pltpu.VMEM),
        scratch_shapes=[
            pltpu.VMEM((levels,) + shard.shape, shard.dtype),
            pltpu.VMEM(shard.shape, shard.dtype),
            pltpu.VMEM((7, levels) + tile, shard.dtype),
            pltpu.SemaphoreType.DMA((2, levels)),
            pltpu.SemaphoreType.DMA((levels,)),
            pltpu.SemaphoreType.DMA((7, levels)),
            pltpu.SemaphoreType.DMA((devices,)),
        ],
        compiler_params=pltpu.CompilerParams(
            collective_id=1, has_side_effects=True, vmem_limit_bytes=32 * 2**20
        ),
    )(slots, shard)


def adam(grad, master, first_moment, second_moment):
    new_first = decay_first * first_moment + (1.0 - decay_first) * grad
    new_second = decay_second * second_moment + (1.0 - decay_second) * grad * grad
    first_hat = new_first / (1.0 - decay_first**step_number)
    second_hat = new_second / (1.0 - decay_second**step_number)
    new_master = master - learn_rate * (
        first_hat / (jnp.sqrt(second_hat) + epsilon) + weight_decay * master
    )
    return new_master, new_first, new_second


def gathered(
    tokens,
    hidden_grad,
    routing,
    row_count,
    old_slots,
    new_slots,
    master,
    first_moment,
    second_moment,
):
    places = lax.axis_size("place")
    groups = lax.axis_size("dp")
    devices = places * groups
    experts, rows_shard, width = master.shape
    half = width // 2
    place_here = lax.axis_index("place")
    group_here = lax.axis_index("dp")
    rows_in = tokens[0, 0]
    rows, depth = rows_in.shape
    order = routing[0, 0]
    batches, batch_rows = order.shape
    turned = rows_in.T.reshape(devices, rows_shard, rows)
    columns = lax.all_to_all(turned, ("dp", "place"), split_axis=0, concat_axis=0, tiled=True)
    weights = expert_rows(master.astype(jnp.bfloat16), old_slots).reshape(depth, width)
    live = jnp.arange(rows, dtype=jnp.int32) < row_count[group_here, place_here]
    place_of = (
        order[:, None, :] == jnp.arange(batch_rows, dtype=jnp.int32)[None, :, None]
    ) & live.reshape(batches, 1, batch_rows)
    incoming = jnp.einsum(
        "mri,mik->mrk",
        place_of.astype(jnp.bfloat16),
        hidden_grad[0, 0].reshape(batches, batch_rows, half),
        preferred_element_type=jnp.float32,
    ).reshape(rows, half)
    both = jnp.dot(rows_in, weights, preferred_element_type=jnp.float32)
    gate = both[:, :half]
    upward = both[:, half:]
    sigma = jax.nn.sigmoid(gate)
    active = gate * sigma
    slope = sigma * (1.0 + gate * (1.0 - sigma))
    local = jnp.concatenate([incoming * upward * slope, incoming * active], axis=1).astype(
        jnp.bfloat16
    )
    all_local = whole_gather(local.reshape(experts, rows * width // (experts * width), width))
    select = old_slots[None, :] == jnp.arange(experts, dtype=jnp.int32)[:, None]
    chosen = jnp.tile(select, (1, groups))
    stacked = jnp.where(
        chosen[:, None, :, None], columns.transpose(1, 0, 2)[None], jnp.bfloat16(0)
    ).reshape(experts * rows_shard, devices * rows)
    grad_sum = jnp.dot(
        stacked, all_local.reshape(devices * rows, width), preferred_element_type=jnp.float32
    ).reshape(experts, rows_shard, width)
    per_slot = jnp.sum(row_count.astype(jnp.float32), axis=0)
    total = jnp.sum(jnp.where(select, per_slot[None, :], 0.0), axis=1)
    grad = grad_sum / total[:, None, None]
    new_master, new_first, new_second = adam(grad, master, first_moment, second_moment)
    new_weights = expert_rows(new_master.astype(jnp.bfloat16), new_slots)
    return (
        new_weights.reshape(1, depth, width),
        new_master,
        new_first,
        new_second,
    )


def fits(mesh):
    return mesh.shape["dp"] == 2 and mesh.shape["place"] in (8, 16)


def solution(mesh):
    placed = (
        P("dp", "place", None, None),
        P("dp", "place", None, None),
        P("dp", "place", None, None),
        P(),
        P(),
        P(),
        P(None, ("dp", "place"), None),
        P(None, ("dp", "place"), None),
        P(None, ("dp", "place"), None),
    )
    return jax.shard_map(
        gathered if fits(mesh) else shards,
        mesh=mesh,
        in_specs=placed,
        out_specs=(
            P("place", None, None),
            P(None, ("dp", "place"), None),
            P(None, ("dp", "place"), None),
            P(None, ("dp", "place"), None),
        ),
        check_vma=False,
    )
```

```python
import functools

import jax
import jax.numpy as jnp
from jax import lax
from jax.experimental import pallas as pl
from jax.experimental.pallas import tpu as pltpu
from jax.sharding import PartitionSpec as P

decay_first = 0.9
decay_second = 0.95
learn_rate = 0.001
weight_decay = 0.1
epsilon = 1e-08
step_number = 20.0


def spread(shard, slots):
    experts, rows_shard, width = shard.shape
    places = lax.axis_size("place")
    select = (slots[:, None] == jnp.arange(experts, dtype=jnp.int32)[None, :]).astype(jnp.bfloat16)
    picked = jnp.dot(
        select, shard.reshape(experts, rows_shard * width), preferred_element_type=jnp.float32
    ).astype(jnp.bfloat16)
    landed = lax.all_to_all(
        picked.reshape(places, rows_shard, width), "place", split_axis=0, concat_axis=0, tiled=True
    )
    whole = lax.all_gather(landed.reshape(places * rows_shard, width), "dp", axis=0, tiled=True)
    return whole


def batch_grad(total, rows_in, grads_in, order, count, weights, start):
    rows = order.shape[0]
    half = weights.shape[1] // 2
    picked = jnp.take(rows_in, start + order, axis=0)
    both = jnp.dot(picked, weights, preferred_element_type=jnp.float32)
    gate = both[:, :half]
    upward = both[:, half:]
    sigma = jax.nn.sigmoid(gate)
    active = gate * sigma
    slope = sigma * (1.0 + gate * (1.0 - sigma))
    live = start + jnp.arange(rows, dtype=jnp.int32) < count
    incoming = jnp.where(live[:, None], grads_in[start : start + rows].astype(jnp.float32), 0.0)
    local = jnp.concatenate([incoming * upward * slope, incoming * active], axis=1).astype(
        jnp.bfloat16
    )
    return total + lax.dot_general(
        picked, local, (((0,), (0,)), ((), ())), preferred_element_type=jnp.float32
    )


def shards(
    tokens,
    hidden_grad,
    routing,
    row_count,
    old_slots,
    new_slots,
    master,
    first_moment,
    second_moment,
):
    places = lax.axis_size("place")
    groups = lax.axis_size("dp")
    experts, rows_shard, width = master.shape
    place_here = lax.axis_index("place")
    group_here = lax.axis_index("dp")
    weights = spread(master.astype(jnp.bfloat16), old_slots)
    rows_in = tokens[0, 0]
    grads_in = hidden_grad[0, 0]
    order = routing[0, 0]
    count = row_count[group_here, place_here]
    batch_rows = order.shape[1]
    summed = jnp.zeros((rows_in.shape[1], width), jnp.float32)
    for batch_index in range(order.shape[0]):
        start = batch_index * batch_rows
        summed = batch_grad(summed, rows_in, grads_in, order[batch_index], count, weights, start)
    select = (old_slots[:, None] == jnp.arange(experts, dtype=jnp.int32)[None, :]).astype(
        jnp.float32
    )
    blocks = summed.reshape(groups, places, rows_shard, width)
    landed = lax.all_to_all(blocks, "place", split_axis=1, concat_axis=1, tiled=True)
    merged = jnp.einsum(
        "se,dsx->dex",
        select,
        landed.reshape(groups, places, rows_shard * width),
        precision=lax.Precision.HIGHEST,
    )
    mine = lax.psum_scatter(merged, "dp", scatter_dimension=0, tiled=True)
    grad_sum = mine.reshape(experts, rows_shard, width)
    per_slot = jnp.sum(row_count.astype(jnp.float32), axis=0)
    total = jnp.dot(per_slot, select, precision=lax.Precision.HIGHEST)
    grad = grad_sum / total[:, None, None]
    new_first = decay_first * first_moment + (1.0 - decay_first) * grad
    new_second = decay_second * second_moment + (1.0 - decay_second) * grad * grad
    first_hat = new_first / (1.0 - decay_first**step_number)
    second_hat = new_second / (1.0 - decay_second**step_number)
    new_master = master - learn_rate * (
        first_hat / (jnp.sqrt(second_hat) + epsilon) + weight_decay * master
    )
    new_weights = spread(new_master.astype(jnp.bfloat16), new_slots)
    return (new_weights[None], new_master, new_first, new_second)


MESH = pl.DeviceIdType.MESH


def spot(places):
    here = lax.axis_index("place")
    return lax.axis_index("dp"), here // 4, (here // 2) % 2, here % 2


def device(y, z, x, c):
    return (y, z * 4 + x * 2 + c)


def meet(partners, z, levels, up, down):
    barrier = pltpu.get_barrier_semaphore()

    def greet(partner):
        pl.semaphore_signal(barrier, inc=1, device_id=partner, device_id_type=MESH)

    for partner in partners:
        greet(partner)
    pl.when(z < levels - 1)(lambda: greet(up))
    pl.when(z > 0)(lambda: greet(down))
    has_down = (z + levels - 2) // (levels - 1)
    has_up = (2 * levels - 3 - z) // (levels - 1)
    pl.semaphore_wait(barrier, len(partners) + has_up + has_down)


def shifts_of(levels):
    steps = [(dy, dz, dx, dc) for dz in range(levels) for dy in (0, 1) for dx in (0, 1) for dc in (0, 1)]
    return steps[1:]


def meet_all(partners):
    barrier = pltpu.get_barrier_semaphore()
    for partner in partners:
        pl.semaphore_signal(barrier, inc=1, device_id=partner, device_id_type=MESH)
    pl.semaphore_wait(barrier, len(partners))


def exchange(places, turned_ref, columns_ref, send_sem, recv_sem):
    levels = places // 4
    y, z, x, c = spot(places)
    mine = y * places + z * 4 + x * 2 + c
    steps = shifts_of(levels)
    partners = [
        device((y + dy) % 2, (z + dz) % levels, (x + dx) % 2, (c + dc) % 2)
        for dy, dz, dx, dc in steps
    ]

    def copy(i, landing):
        there = partners[i][0] * places + partners[i][1]
        return remote(
            turned_ref.at[there],
            columns_ref.at[landing],
            send_sem.at[i],
            recv_sem.at[landing],
            partners[i],
        )

    def start(dz):
        for i, step in enumerate(steps):
            if step[1] == dz:
                copy(i, mine).start()

    def end():
        for i, partner in enumerate(partners):
            copy(i, partner[0] * places + partner[1]).wait_recv()
            copy(i, mine).wait_send()

    return partners, mine, start, end


def remote(source, target, send_sem, recv_sem, partner):
    return pltpu.make_async_remote_copy(
        src_ref=source,
        dst_ref=target,
        send_sem=send_sem,
        recv_sem=recv_sem,
        device_id=partner,
        device_id_type=MESH,
    )


def gather_kernel(
    places, own_ref, turned_ref, all_ref, columns_ref, send_sem, recv_sem, own_sem, turn_send, turn_recv
):
    levels = places // 4
    y, z, x, c = spot(places)

    def block(y, z, x, c):
        return y * places + z * 4 + x * 2 + c

    x_first, y_first = (x + 1 - c) % 2, (y + c) % 2
    x_last, y_last = (x + c) % 2, (y + 1 - c) % 2
    up, down = device(y, z + 1, x, c), device(y, z - 1, x, c)
    first = device(y_first, z, x_first, c)
    last = device(y_last, z, x_last, c)
    sibling = device(y, z, x, 1 - c)
    everyone, mine, turn, turned = exchange(places, turned_ref, columns_ref, turn_send, turn_recv)
    meet_all(everyone)

    def copy(kind, level, index, partner, source=None):
        return remote(
            all_ref.at[index] if source is None else source,
            all_ref.at[index],
            send_sem.at[kind, level],
            recv_sem.at[index],
            partner,
        )

    def arrived(index):
        copy(0, 0, index, sibling).wait_recv()

    pl.when(z < levels - 1)(lambda: copy(0, z, mine, up, own_ref).start())
    pl.when(z > 0)(lambda: copy(1, z, mine, down, own_ref).start())
    copy(2, z, mine, first, own_ref).start()
    copy(3, z, mine, last, own_ref).start()
    copy(4, z, mine, sibling, own_ref).start()
    keep = pltpu.make_async_copy(own_ref, all_ref.at[mine], own_sem)
    keep.start()
    columns_ref[mine] = turned_ref[mine]

    def straight(level, below):
        index = block(y, level, x, c)
        arrived(index)
        if below:
            pl.when(z < levels - 1)(lambda: copy(0, level, index, up).start())
        else:
            pl.when(z > 0)(lambda: copy(1, level, index, down).start())
        copy(2, level, index, first).start()
        copy(3, level, index, last).start()
        copy(4, level, index, sibling).start()

    def over(level, below):
        index = block(y_first, level, x_first, c)
        arrived(index)
        copy(5, level, index, last).start()
        copy(6, level, index, sibling).start()

    def both_ways(k, visit):
        if k == 0:
            visit(z, True)
        else:
            pl.when(z >= k)(lambda: visit(z - k, True))
            pl.when(z < levels - k)(lambda: visit(z + k, False))

    for k in range(1, levels):
        both_ways(k, straight)
        both_ways(k - 1, over)
        turn(k)
    both_ways(levels - 1, over)
    turn(0)

    def ending(level, below):
        for kind, index in ((7, block(y_last, level, x_last, c)), (8, block(1 - y, level, 1 - x, c))):
            arrived(index)
            copy(kind, level, index, sibling).start()

    for k in range(levels):
        both_ways(k, ending)
    for level in range(levels):
        for side in range(2):
            for group in range(2):
                arrived(block(group, level, side, 1 - c))
    keep.wait()
    turned()
    for level in range(levels):
        for kind in range(2, 9):
            copy(kind, level, mine, sibling).wait_send()
        pl.when((z >= level) & (z < levels - 1))(
            lambda level=level: copy(0, level, mine, sibling).wait_send()
        )
        pl.when((z <= level) & (z > 0))(
            lambda level=level: copy(1, level, mine, sibling).wait_send()
        )


def whole_gather(shard, turned):
    places = lax.axis_size("place")
    devices = lax.axis_size("dp") * places
    levels = places // 4
    return pl.pallas_call(
        functools.partial(gather_kernel, places),
        out_shape=(
            jax.ShapeDtypeStruct((devices,) + shard.shape, shard.dtype),
            jax.ShapeDtypeStruct(turned.shape, turned.dtype),
        ),
        in_specs=[pl.BlockSpec(memory_space=pl.ANY), pl.BlockSpec(memory_space=pltpu.VMEM)],
        out_specs=(pl.BlockSpec(memory_space=pl.ANY), pl.BlockSpec(memory_space=pltpu.VMEM)),
        scratch_shapes=[
            pltpu.SemaphoreType.DMA((9, levels)),
            pltpu.SemaphoreType.DMA((devices,)),
            pltpu.SemaphoreType.DMA,
            pltpu.SemaphoreType.DMA((devices,)),
            pltpu.SemaphoreType.DMA((devices,)),
        ],
        compiler_params=pltpu.CompilerParams(
            collective_id=0, has_side_effects=True, vmem_limit_bytes=32 * 2**20
        ),
    )(shard, turned)


def expert_kernel(places, turning, slots_ref, own_ref, *refs):
    if turning:
        turned_ref, out_ref, columns_ref, *refs = refs
    else:
        out_ref, *refs = refs
    line, held, picked, line_send, line_recv, send_sem, recv_sem, *refs = refs
    levels = places // 4
    y, z, x, c = spot(places)
    up, down = device(y, z + 1, x, c), device(y, z - 1, x, c)
    shifts = [(0, 1, 0), (1, 0, 0), (0, 1, 1), (1, 0, 1), (1, 1, 0), (1, 1, 1), (0, 0, 1)]
    plane = [((y + dy) % 2, (x + dx) % 2, (c + dc) % 2) for dy, dx, dc in shifts]
    partners = [device(there_y, z, there_x, there_c) for there_y, there_x, there_c in plane]
    line[z] = own_ref[...]
    if turning:
        everyone, mine, turn, turned = exchange(places, turned_ref, columns_ref, *refs)
        meet_all(everyone)
    else:
        meet(partners, z, levels, up, down)

    def pass_on(way, level):
        return remote(
            line.at[level],
            line.at[level],
            line_send.at[way, level],
            line_recv.at[level],
            (up, down)[way],
        )

    def hand(j, level, index):
        return remote(
            picked.at[j, level],
            out_ref.at[index],
            send_sem.at[j, level],
            recv_sem.at[index],
            partners[j],
        )

    def fan(level):
        index = y * places + level * 4 + x * 2 + c
        held[...] = line[level]
        for j, partner in enumerate(partners):
            picked[j, level] = held[slots_ref[partner[1]]]
            hand(j, level, index).start()
        out_ref[index] = held[slots_ref[z * 4 + x * 2 + c]]

    pl.when(z < levels - 1)(lambda: pass_on(0, z).start())
    pl.when(z > 0)(lambda: pass_on(1, z).start())
    fan(z)

    def below(level):
        pass_on(0, level).wait_recv()
        pl.when(z < levels - 1)(lambda: pass_on(0, level).start())
        fan(level)

    def above(level):
        pass_on(1, level).wait_recv()
        pl.when(z > 0)(lambda: pass_on(1, level).start())
        fan(level)

    for k in range(1, levels):
        pl.when(z >= k)(lambda k=k: below(z - k))
        pl.when(z < levels - k)(lambda k=k: above(z + k))
        if turning:
            turn(k)
    if turning:
        turn(0)
        columns_ref[mine] = turned_ref[mine]
        turned()
    for level in range(levels):
        for j, (there_y, there_x, there_c) in enumerate(plane):
            hand(j, level, there_y * places + level * 4 + there_x * 2 + there_c).wait()
        pl.when((z >= level) & (z < levels - 1))(lambda level=level: pass_on(0, level).wait_send())
        pl.when((z <= level) & (z > 0))(lambda level=level: pass_on(1, level).wait_send())


def expert_rows(shard, slots, turned=None):
    places = lax.axis_size("place")
    devices = lax.axis_size("dp") * places
    levels = places // 4
    tile = shard.shape[1:]
    turning = turned is not None
    extra = [turned] if turning else []
    vmem = pl.BlockSpec(memory_space=pltpu.VMEM)
    return pl.pallas_call(
        functools.partial(expert_kernel, places, turning),
        out_shape=[jax.ShapeDtypeStruct((devices,) + tile, shard.dtype)]
        + [jax.ShapeDtypeStruct(array.shape, array.dtype) for array in extra],
        in_specs=[pl.BlockSpec(memory_space=pltpu.SMEM), vmem] + [vmem for _ in extra],
        out_specs=[vmem] + [vmem for _ in extra],
        scratch_shapes=[
            pltpu.VMEM((levels,) + shard.shape, shard.dtype),
            pltpu.VMEM(shard.shape, shard.dtype),
            pltpu.VMEM((7, levels) + tile, shard.dtype),
            pltpu.SemaphoreType.DMA((2, levels)),
            pltpu.SemaphoreType.DMA((levels,)),
            pltpu.SemaphoreType.DMA((7, levels)),
            pltpu.SemaphoreType.DMA((devices,)),
        ]
        + [pltpu.SemaphoreType.DMA((devices,)) for _ in range(2 * len(extra))],
        compiler_params=pltpu.CompilerParams(
            collective_id=1 + turning, has_side_effects=True, vmem_limit_bytes=32 * 2**20
        ),
    )(slots, shard, *extra)


def adam(grad, master, first_moment, second_moment):
    new_first = decay_first * first_moment + (1.0 - decay_first) * grad
    new_second = decay_second * second_moment + (1.0 - decay_second) * grad * grad
    first_hat = new_first / (1.0 - decay_first**step_number)
    second_hat = new_second / (1.0 - decay_second**step_number)
    new_master = master - learn_rate * (
        first_hat / (jnp.sqrt(second_hat) + epsilon) + weight_decay * master
    )
    return new_master, new_first, new_second


def gathered(
    tokens,
    hidden_grad,
    routing,
    row_count,
    old_slots,
    new_slots,
    master,
    first_moment,
    second_moment,
):
    places = lax.axis_size("place")
    groups = lax.axis_size("dp")
    devices = places * groups
    experts, rows_shard, width = master.shape
    half = width // 2
    place_here = lax.axis_index("place")
    group_here = lax.axis_index("dp")
    rows_in = tokens[0, 0]
    rows, depth = rows_in.shape
    order = routing[0, 0]
    batches, batch_rows = order.shape
    turned = rows_in.reshape(rows, devices, 2, rows_shard // 2).transpose(2, 1, 3, 0)
    weights, upper = expert_rows(master.astype(jnp.bfloat16), old_slots, turned[0])
    weights = weights.reshape(depth, width)
    live = jnp.arange(rows, dtype=jnp.int32) < row_count[group_here, place_here]
    place_of = (
        order[:, None, :] == jnp.arange(batch_rows, dtype=jnp.int32)[None, :, None]
    ) & live.reshape(batches, 1, batch_rows)
    incoming = jnp.einsum(
        "mri,mik->mrk",
        place_of.astype(jnp.bfloat16),
        hidden_grad[0, 0].reshape(batches, batch_rows, half),
        preferred_element_type=jnp.float32,
    ).reshape(rows, half)
    both = jnp.dot(rows_in, weights, preferred_element_type=jnp.float32)
    gate = both[:, :half]
    upward = both[:, half:]
    sigma = jax.nn.sigmoid(gate)
    active = gate * sigma
    slope = sigma * (1.0 + gate * (1.0 - sigma))
    local = jnp.concatenate([incoming * upward * slope, incoming * active], axis=1).astype(
        jnp.bfloat16
    )
    all_local, lower = whole_gather(local, turned[1])
    columns = jnp.concatenate([upper.transpose(1, 0, 2), lower.transpose(1, 0, 2)], axis=0)
    select = old_slots[None, :] == jnp.arange(experts, dtype=jnp.int32)[:, None]
    chosen = jnp.tile(select, (1, groups))
    stacked = jnp.where(
        chosen[:, None, :, None], columns[None], jnp.bfloat16(0)
    ).reshape(experts * rows_shard, devices * rows)
    grad_sum = jnp.dot(
        stacked, all_local.reshape(devices * rows, width), preferred_element_type=jnp.float32
    ).reshape(experts, rows_shard, width)
    per_slot = jnp.sum(row_count.astype(jnp.float32), axis=0)
    total = jnp.sum(jnp.where(select, per_slot[None, :], 0.0), axis=1)
    grad = grad_sum / total[:, None, None]
    new_master, new_first, new_second = adam(grad, master, first_moment, second_moment)
    (new_weights,) = expert_rows(new_master.astype(jnp.bfloat16), new_slots)
    return (
        new_weights.reshape(1, depth, width),
        new_master,
        new_first,
        new_second,
    )


def fits(mesh):
    return mesh.shape["dp"] == 2 and mesh.shape["place"] in (8, 16)


def solution(mesh):
    placed = (
        P("dp", "place", None, None),
        P("dp", "place", None, None),
        P("dp", "place", None, None),
        P(),
        P(),
        P(),
        P(None, ("dp", "place"), None),
        P(None, ("dp", "place"), None),
        P(None, ("dp", "place"), None),
    )
    return jax.shard_map(
        gathered if fits(mesh) else shards,
        mesh=mesh,
        in_specs=placed,
        out_specs=(
            P("place", None, None),
            P(None, ("dp", "place"), None),
            P(None, ("dp", "place"), None),
            P(None, ("dp", "place"), None),
        ),
        check_vma=False,
    )
```

```python
import functools

import jax
import jax.numpy as jnp
from jax import lax
from jax.experimental import pallas as pl
from jax.experimental.pallas import tpu as pltpu
from jax.sharding import PartitionSpec as P

decay_first = 0.9
decay_second = 0.95
learn_rate = 0.001
weight_decay = 0.1
epsilon = 1e-08
step_number = 20.0


def spread(shard, slots):
    experts, rows_shard, width = shard.shape
    places = lax.axis_size("place")
    select = (slots[:, None] == jnp.arange(experts, dtype=jnp.int32)[None, :]).astype(jnp.bfloat16)
    picked = jnp.dot(
        select, shard.reshape(experts, rows_shard * width), preferred_element_type=jnp.float32
    ).astype(jnp.bfloat16)
    landed = lax.all_to_all(
        picked.reshape(places, rows_shard, width), "place", split_axis=0, concat_axis=0, tiled=True
    )
    whole = lax.all_gather(landed.reshape(places * rows_shard, width), "dp", axis=0, tiled=True)
    return whole


def batch_grad(total, rows_in, grads_in, order, count, weights, start):
    rows = order.shape[0]
    half = weights.shape[1] // 2
    picked = jnp.take(rows_in, start + order, axis=0)
    both = jnp.dot(picked, weights, preferred_element_type=jnp.float32)
    gate = both[:, :half]
    upward = both[:, half:]
    sigma = jax.nn.sigmoid(gate)
    active = gate * sigma
    slope = sigma * (1.0 + gate * (1.0 - sigma))
    live = start + jnp.arange(rows, dtype=jnp.int32) < count
    incoming = jnp.where(live[:, None], grads_in[start : start + rows].astype(jnp.float32), 0.0)
    local = jnp.concatenate([incoming * upward * slope, incoming * active], axis=1).astype(
        jnp.bfloat16
    )
    return total + lax.dot_general(
        picked, local, (((0,), (0,)), ((), ())), preferred_element_type=jnp.float32
    )


def shards(
    tokens,
    hidden_grad,
    routing,
    row_count,
    old_slots,
    new_slots,
    master,
    first_moment,
    second_moment,
):
    places = lax.axis_size("place")
    groups = lax.axis_size("dp")
    experts, rows_shard, width = master.shape
    place_here = lax.axis_index("place")
    group_here = lax.axis_index("dp")
    weights = spread(master.astype(jnp.bfloat16), old_slots)
    rows_in = tokens[0, 0]
    grads_in = hidden_grad[0, 0]
    order = routing[0, 0]
    count = row_count[group_here, place_here]
    batch_rows = order.shape[1]
    summed = jnp.zeros((rows_in.shape[1], width), jnp.float32)
    for batch_index in range(order.shape[0]):
        start = batch_index * batch_rows
        summed = batch_grad(summed, rows_in, grads_in, order[batch_index], count, weights, start)
    select = (old_slots[:, None] == jnp.arange(experts, dtype=jnp.int32)[None, :]).astype(
        jnp.float32
    )
    blocks = summed.reshape(groups, places, rows_shard, width)
    landed = lax.all_to_all(blocks, "place", split_axis=1, concat_axis=1, tiled=True)
    merged = jnp.einsum(
        "se,dsx->dex",
        select,
        landed.reshape(groups, places, rows_shard * width),
        precision=lax.Precision.HIGHEST,
    )
    mine = lax.psum_scatter(merged, "dp", scatter_dimension=0, tiled=True)
    grad_sum = mine.reshape(experts, rows_shard, width)
    per_slot = jnp.sum(row_count.astype(jnp.float32), axis=0)
    total = jnp.dot(per_slot, select, precision=lax.Precision.HIGHEST)
    grad = grad_sum / total[:, None, None]
    new_first = decay_first * first_moment + (1.0 - decay_first) * grad
    new_second = decay_second * second_moment + (1.0 - decay_second) * grad * grad
    first_hat = new_first / (1.0 - decay_first**step_number)
    second_hat = new_second / (1.0 - decay_second**step_number)
    new_master = master - learn_rate * (
        first_hat / (jnp.sqrt(second_hat) + epsilon) + weight_decay * master
    )
    new_weights = spread(new_master.astype(jnp.bfloat16), new_slots)
    return (new_weights[None], new_master, new_first, new_second)


MESH = pl.DeviceIdType.MESH


def spot(places):
    here = lax.axis_index("place")
    return lax.axis_index("dp"), here // 4, (here // 2) % 2, here % 2


def device(y, z, x, c):
    return (y, z * 4 + x * 2 + c)


def meet(partners, z, levels, up, down):
    barrier = pltpu.get_barrier_semaphore()

    def greet(partner):
        pl.semaphore_signal(barrier, inc=1, device_id=partner, device_id_type=MESH)

    for partner in partners:
        greet(partner)
    pl.when(z < levels - 1)(lambda: greet(up))
    pl.when(z > 0)(lambda: greet(down))
    has_down = (z + levels - 2) // (levels - 1)
    has_up = (2 * levels - 3 - z) // (levels - 1)
    pl.semaphore_wait(barrier, len(partners) + has_up + has_down)


def shifts_of(levels):
    steps = [(dy, dz, dx, dc) for dz in range(levels) for dy in (0, 1) for dx in (0, 1) for dc in (0, 1)]
    return steps[1:]


def meet_all(partners):
    barrier = pltpu.get_barrier_semaphore()
    for partner in partners:
        pl.semaphore_signal(barrier, inc=1, device_id=partner, device_id_type=MESH)
    pl.semaphore_wait(barrier, len(partners))


def exchange(places, turned_ref, columns_ref, send_sem, recv_sem):
    levels = places // 4
    y, z, x, c = spot(places)
    mine = y * places + z * 4 + x * 2 + c
    steps = shifts_of(levels)
    partners = [
        device((y + dy) % 2, (z + dz) % levels, (x + dx) % 2, (c + dc) % 2)
        for dy, dz, dx, dc in steps
    ]

    def copy(i, landing):
        there = partners[i][0] * places + partners[i][1]
        return remote(
            turned_ref.at[there],
            columns_ref.at[landing],
            send_sem.at[i],
            recv_sem.at[landing],
            partners[i],
        )

    def start(dz):
        for i, step in enumerate(steps):
            if step[1] == dz:
                copy(i, mine).start()

    def end():
        for i, partner in enumerate(partners):
            copy(i, partner[0] * places + partner[1]).wait_recv()
            copy(i, mine).wait_send()

    return partners, mine, start, end


def remote(source, target, send_sem, recv_sem, partner):
    return pltpu.make_async_remote_copy(
        src_ref=source,
        dst_ref=target,
        send_sem=send_sem,
        recv_sem=recv_sem,
        device_id=partner,
        device_id_type=MESH,
    )


def gather_kernel(
    places, own_ref, turned_ref, all_ref, columns_ref, send_sem, recv_sem, own_sem, turn_send, turn_recv
):
    levels = places // 4
    y, z, x, c = spot(places)

    def block(y, z, x, c):
        return y * places + z * 4 + x * 2 + c

    x_first, y_first = (x + 1 - c) % 2, (y + c) % 2
    x_last, y_last = (x + c) % 2, (y + 1 - c) % 2
    up, down = device(y, z + 1, x, c), device(y, z - 1, x, c)
    first = device(y_first, z, x_first, c)
    last = device(y_last, z, x_last, c)
    sibling = device(y, z, x, 1 - c)
    everyone, mine, turn, turned = exchange(places, turned_ref, columns_ref, turn_send, turn_recv)
    meet_all(everyone)

    def copy(kind, level, index, partner, source=None):
        return remote(
            all_ref.at[index] if source is None else source,
            all_ref.at[index],
            send_sem.at[kind, level],
            recv_sem.at[index],
            partner,
        )

    def arrived(index):
        copy(0, 0, index, sibling).wait_recv()

    pl.when(z < levels - 1)(lambda: copy(0, z, mine, up, own_ref).start())
    pl.when(z > 0)(lambda: copy(1, z, mine, down, own_ref).start())
    copy(2, z, mine, first, own_ref).start()
    copy(3, z, mine, last, own_ref).start()
    copy(4, z, mine, sibling, own_ref).start()
    keep = pltpu.make_async_copy(own_ref, all_ref.at[mine], own_sem)
    keep.start()
    columns_ref[mine] = turned_ref[mine]

    def straight(level, below):
        index = block(y, level, x, c)
        arrived(index)
        if below:
            pl.when(z < levels - 1)(lambda: copy(0, level, index, up).start())
        else:
            pl.when(z > 0)(lambda: copy(1, level, index, down).start())
        copy(2, level, index, first).start()
        copy(3, level, index, last).start()
        copy(4, level, index, sibling).start()

    def over(level, below):
        index = block(y_first, level, x_first, c)
        arrived(index)
        copy(5, level, index, last).start()
        copy(6, level, index, sibling).start()

    def both_ways(k, visit):
        if k == 0:
            visit(z, True)
        else:
            pl.when(z >= k)(lambda: visit(z - k, True))
            pl.when(z < levels - k)(lambda: visit(z + k, False))

    for k in range(1, levels):
        both_ways(k, straight)
        both_ways(k - 1, over)
        turn(k)
    both_ways(levels - 1, over)
    turn(0)

    def ending(level, below):
        for kind, index in ((7, block(y_last, level, x_last, c)), (8, block(1 - y, level, 1 - x, c))):
            arrived(index)
            copy(kind, level, index, sibling).start()

    for k in range(levels):
        both_ways(k, ending)
    for level in range(levels):
        for side in range(2):
            for group in range(2):
                arrived(block(group, level, side, 1 - c))
    keep.wait()
    turned()
    for level in range(levels):
        for kind in range(2, 9):
            copy(kind, level, mine, sibling).wait_send()
        pl.when((z >= level) & (z < levels - 1))(
            lambda level=level: copy(0, level, mine, sibling).wait_send()
        )
        pl.when((z <= level) & (z > 0))(
            lambda level=level: copy(1, level, mine, sibling).wait_send()
        )


def whole_gather(shard, turned):
    places = lax.axis_size("place")
    devices = lax.axis_size("dp") * places
    levels = places // 4
    return pl.pallas_call(
        functools.partial(gather_kernel, places),
        out_shape=(
            jax.ShapeDtypeStruct((devices,) + shard.shape, shard.dtype),
            jax.ShapeDtypeStruct(turned.shape, turned.dtype),
        ),
        in_specs=[pl.BlockSpec(memory_space=pl.ANY), pl.BlockSpec(memory_space=pltpu.VMEM)],
        out_specs=(pl.BlockSpec(memory_space=pl.ANY), pl.BlockSpec(memory_space=pltpu.VMEM)),
        scratch_shapes=[
            pltpu.SemaphoreType.DMA((9, levels)),
            pltpu.SemaphoreType.DMA((devices,)),
            pltpu.SemaphoreType.DMA,
            pltpu.SemaphoreType.DMA((devices,)),
            pltpu.SemaphoreType.DMA((devices,)),
        ],
        compiler_params=pltpu.CompilerParams(
            collective_id=0, has_side_effects=True, vmem_limit_bytes=32 * 2**20
        ),
    )(shard, turned)


def expert_kernel(places, turning, slots_ref, own_ref, *refs):
    if turning:
        turned_ref, out_ref, columns_ref, *refs = refs
    else:
        out_ref, *refs = refs
    line, held, picked, line_send, line_recv, send_sem, recv_sem, *refs = refs
    levels = places // 4
    y, z, x, c = spot(places)
    up, down = device(y, z + 1, x, c), device(y, z - 1, x, c)
    shifts = [(0, 1, 0), (1, 0, 0), (0, 1, 1), (1, 0, 1), (1, 1, 0), (1, 1, 1), (0, 0, 1)]
    plane = [((y + dy) % 2, (x + dx) % 2, (c + dc) % 2) for dy, dx, dc in shifts]
    partners = [device(there_y, z, there_x, there_c) for there_y, there_x, there_c in plane]
    line[z] = own_ref[...].astype(line.dtype)
    if turning:
        everyone, mine, turn, turned = exchange(places, turned_ref, columns_ref, *refs)
        meet_all(everyone)
    else:
        meet(partners, z, levels, up, down)

    def pass_on(way, level):
        return remote(
            line.at[level],
            line.at[level],
            line_send.at[way, level],
            line_recv.at[level],
            (up, down)[way],
        )

    def hand(j, level, index):
        return remote(
            picked.at[j, level],
            out_ref.at[index],
            send_sem.at[j, level],
            recv_sem.at[index],
            partners[j],
        )

    def fan(level):
        index = y * places + level * 4 + x * 2 + c
        held[...] = line[level]
        for j, partner in enumerate(partners):
            picked[j, level] = held[slots_ref[partner[1]]]
            hand(j, level, index).start()
        out_ref[index] = held[slots_ref[z * 4 + x * 2 + c]]

    pl.when(z < levels - 1)(lambda: pass_on(0, z).start())
    pl.when(z > 0)(lambda: pass_on(1, z).start())
    fan(z)

    def below(level):
        pass_on(0, level).wait_recv()
        pl.when(z < levels - 1)(lambda: pass_on(0, level).start())
        fan(level)

    def above(level):
        pass_on(1, level).wait_recv()
        pl.when(z > 0)(lambda: pass_on(1, level).start())
        fan(level)

    for k in range(1, levels):
        pl.when(z >= k)(lambda k=k: below(z - k))
        pl.when(z < levels - k)(lambda k=k: above(z + k))
        if turning:
            turn(k)
    if turning:
        turn(0)
        columns_ref[mine] = turned_ref[mine]
        turned()
    for level in range(levels):
        for j, (there_y, there_x, there_c) in enumerate(plane):
            hand(j, level, there_y * places + level * 4 + there_x * 2 + there_c).wait()
        pl.when((z >= level) & (z < levels - 1))(lambda level=level: pass_on(0, level).wait_send())
        pl.when((z <= level) & (z > 0))(lambda level=level: pass_on(1, level).wait_send())


def expert_rows(shard, slots, turned=None):
    places = lax.axis_size("place")
    devices = lax.axis_size("dp") * places
    levels = places // 4
    tile = shard.shape[1:]
    turning = turned is not None
    extra = [turned] if turning else []
    vmem = pl.BlockSpec(memory_space=pltpu.VMEM)
    return pl.pallas_call(
        functools.partial(expert_kernel, places, turning),
        out_shape=[jax.ShapeDtypeStruct((devices,) + tile, jnp.bfloat16)]
        + [jax.ShapeDtypeStruct(array.shape, array.dtype) for array in extra],
        in_specs=[pl.BlockSpec(memory_space=pltpu.SMEM), vmem] + [vmem for _ in extra],
        out_specs=[vmem] + [vmem for _ in extra],
        scratch_shapes=[
            pltpu.VMEM((levels,) + shard.shape, jnp.bfloat16),
            pltpu.VMEM(shard.shape, jnp.bfloat16),
            pltpu.VMEM((7, levels) + tile, jnp.bfloat16),
            pltpu.SemaphoreType.DMA((2, levels)),
            pltpu.SemaphoreType.DMA((levels,)),
            pltpu.SemaphoreType.DMA((7, levels)),
            pltpu.SemaphoreType.DMA((devices,)),
        ]
        + [pltpu.SemaphoreType.DMA((devices,)) for _ in range(2 * len(extra))],
        compiler_params=pltpu.CompilerParams(
            collective_id=1 + turning, has_side_effects=True, vmem_limit_bytes=32 * 2**20
        ),
    )(slots, shard, *extra)


def adam(grad, master, first_moment, second_moment):
    new_first = decay_first * first_moment + (1.0 - decay_first) * grad
    new_second = decay_second * second_moment + (1.0 - decay_second) * grad * grad
    first_hat = new_first / (1.0 - decay_first**step_number)
    second_hat = new_second / (1.0 - decay_second**step_number)
    new_master = master - learn_rate * (
        first_hat / (jnp.sqrt(second_hat) + epsilon) + weight_decay * master
    )
    return new_master, new_first, new_second


def gathered(
    tokens,
    hidden_grad,
    routing,
    row_count,
    old_slots,
    new_slots,
    master,
    first_moment,
    second_moment,
):
    places = lax.axis_size("place")
    groups = lax.axis_size("dp")
    devices = places * groups
    experts, rows_shard, width = master.shape
    half = width // 2
    place_here = lax.axis_index("place")
    group_here = lax.axis_index("dp")
    rows_in = tokens[0, 0]
    rows, depth = rows_in.shape
    order = routing[0, 0]
    batches, batch_rows = order.shape
    turned = rows_in.reshape(rows, devices, 2, rows_shard // 2).transpose(2, 1, 3, 0)
    weights, upper = expert_rows(master, old_slots, turned[0])
    weights = weights.reshape(depth, width)
    live = jnp.arange(rows, dtype=jnp.int32) < row_count[group_here, place_here]
    place_of = (
        order[:, None, :] == jnp.arange(batch_rows, dtype=jnp.int32)[None, :, None]
    ) & live.reshape(batches, 1, batch_rows)
    incoming = jnp.einsum(
        "mri,mik->mrk",
        place_of.astype(jnp.bfloat16),
        hidden_grad[0, 0].reshape(batches, batch_rows, half),
        preferred_element_type=jnp.float32,
    ).reshape(rows, half)
    both = jnp.dot(rows_in, weights, preferred_element_type=jnp.float32)
    gate = both[:, :half]
    upward = both[:, half:]
    sigma = jax.nn.sigmoid(gate)
    active = gate * sigma
    slope = sigma * (1.0 + gate * (1.0 - sigma))
    local = jnp.concatenate([incoming * upward * slope, incoming * active], axis=1).astype(
        jnp.bfloat16
    )
    all_local, lower = whole_gather(local, turned[1])
    columns = jnp.concatenate([upper.transpose(1, 0, 2), lower.transpose(1, 0, 2)], axis=0)
    select = old_slots[None, :] == jnp.arange(experts, dtype=jnp.int32)[:, None]
    chosen = jnp.tile(select, (1, groups))
    stacked = jnp.where(
        chosen[:, None, :, None], columns[None], jnp.bfloat16(0)
    ).reshape(experts * rows_shard, devices * rows)
    grad_sum = jnp.dot(
        stacked, all_local.reshape(devices * rows, width), preferred_element_type=jnp.float32
    ).reshape(experts, rows_shard, width)
    counts = row_count.astype(jnp.float32)
    total = jnp.sum(jnp.where(select[:, None, :], counts[None], 0.0), axis=(1, 2))
    grad = grad_sum / total[:, None, None]
    new_master, new_first, new_second = adam(grad, master, first_moment, second_moment)
    (new_weights,) = expert_rows(new_master, new_slots)
    return (
        new_weights.reshape(1, depth, width),
        new_master,
        new_first,
        new_second,
    )


def fits(mesh):
    return mesh.shape["dp"] == 2 and mesh.shape["place"] in (8, 16)


def solution(mesh):
    placed = (
        P("dp", "place", None, None),
        P("dp", "place", None, None),
        P("dp", "place", None, None),
        P(),
        P(),
        P(),
        P(None, ("dp", "place"), None),
        P(None, ("dp", "place"), None),
        P(None, ("dp", "place"), None),
    )
    return jax.shard_map(
        gathered if fits(mesh) else shards,
        mesh=mesh,
        in_specs=placed,
        out_specs=(
            P("place", None, None),
            P(None, ("dp", "place"), None),
            P(None, ("dp", "place"), None),
            P(None, ("dp", "place"), None),
        ),
        check_vma=False,
    )
```
